32 devices in a mesh: lat: 8 (over z, x), lev: 4 (over y, core).
Axes of the slice: x: 2, y: 2, z: 4, core: 2. Of those that a mesh axis runs over, the one named last changes fastest.
Arguments:
- thickness: float32 [8, 128, 1440], P('lev', 'lat'), may hold values from 0.5 to 1.5
- tracers: float32 [8, 8, 128, 1440], P(None, 'lev', 'lat'), may hold values from 0 to 1
- east_courant: float32 [8, 128, 1440], P('lev', 'lat'), may hold values from -1.75 to 1.75
- north_courant: float32 [8, 128, 1440], P('lev', 'lat'), may hold values from -1.75 to 1.75
- vert_courant: float32 [8, 128, 1440], P('lev', 'lat'), may hold values from -1.75 to 1.75
- filter_flags: int32 [128], replicated, may hold values from 0 to 1, as said below
- owner_slots: int32 [128], replicated, may hold values from -1 to 71, as said below
Outputs:
- new_thickness: float32 [8, 128, 1440], P('lev', 'lat')
- new_tracer_mass: float32 [8, 8, 128, 1440], P(None, 'lev', 'lat')
- slot_spectra: float32 [72, 8, 1440], P('lat', 'lev')
The draws below stay inside these ranges and needn't reach their ends.
Inputs may be any that keep to these rules, and one draw needn't show every extreme that they name: `filter_flags`: exactly 72 rows are 1, among them the first 16 and the last 16 rows. `owner_slots`: -1 on rows with flag 0; the flagged rows hold distinct slots covering 0 to 71; slot s is owned by lat index s // 9; the flagged rows of one lat index have at most 2 slots with one owner, and some lat index has exactly 2 with some owner.
All inputs are finite; a program needn't handle non-finite values.
Results may differ from the reference program's by a relative error of at most 0.000076.
Values sent between devices are 32-bit elements; how exact they have to be, the bound alone decides.
A program may use at most 128 MiB of HBM per device.

```python
import math
import jax
import jax.numpy as jnp
from jax import lax

NLON = 1440
NTRAC = 8
LAT_DEV = 16
SLOT_DEV = 9
NLAT = 128
LEVELS = 8
FILTER_ROWS = 72


def polar_flags(key):
    jitter_key = jax.random.fold_in(key, 11)
    row_ids = jnp.arange(NLAT, dtype=jnp.int32)
    distance = jnp.abs(2 * row_ids - (NLAT - 1))
    jitter = jax.random.randint(jitter_key, (NLAT,), 0, 4 * LAT_DEV, dtype=jnp.int32)
    edge = ((row_ids < LAT_DEV) | (row_ids >= NLAT - LAT_DEV)).astype(jnp.int32)
    score = (2 * distance + jitter + edge * (8 * NLAT)) * NLAT + row_ids
    order = jnp.argsort(-score, stable=True)
    chosen = order[:FILTER_ROWS]
    return jnp.zeros((NLAT,), jnp.int32).at[chosen].set(1)


def draw_filter_flags(key, part):
    flags_all = polar_flags(key)
    return flags_all


def draw_owner_slots(key, part):
    flags_all = polar_flags(key)
    key = jax.random.fold_in(key, 5)
    offset = jax.random.randint(key, (), 0, FILTER_ROWS, dtype=jnp.int32)
    ranks = jnp.cumsum(flags_all) - 1
    dealt = (ranks + offset) % FILTER_ROWS
    lat_count = NLAT // LAT_DEV
    slots = dealt % lat_count * SLOT_DEV + dealt // lat_count
    return jnp.where(flags_all == 1, slots, -1).astype(jnp.int32)


def shard_levels(stream_key, dims, pieces, low, high):
    level = 1.0
    for axis_at, blocks in pieces:
        steps = jax.random.uniform(jax.random.fold_in(jax.random.fold_in(stream_key, 6), axis_at), (blocks,), jnp.float32, low / len(pieces), high / len(pieces))
        level = level * jnp.repeat(jnp.exp(steps), dims[axis_at] // blocks).reshape((-1,) + (1,) * (len(dims) - 1 - axis_at))
    return level


def noise(stream_key, shape, width, bound, cuts=(), kind=jnp.bfloat16):
    level = shard_levels(stream_key, shape, cuts, -0.22, 0.18) if cuts else 1.0
    array = jax.random.normal(stream_key, shape, jnp.float32) * width * level
    return jnp.minimum(jnp.maximum(array, -bound), bound).astype(kind)


def setup_inputs(seed: int = 0) -> dict:
    seeds = jax.random.split(jax.random.key(seed), 8)
    thickness = jnp.clip(0.5 + 1.0 * jax.random.uniform(seeds[0], (LEVELS, NLAT, NLON), jnp.float32) ** shard_levels(seeds[0], (LEVELS, NLAT, NLON), ((0, 4), (1, 8)), -0.2, 0.2), 0.5, 1.5)
    tracers = jnp.clip(1.0 * jax.random.uniform(seeds[1], (NTRAC, LEVELS, NLAT, NLON), jnp.float32) ** shard_levels(seeds[1], (NTRAC, LEVELS, NLAT, NLON), ((1, 4), (2, 8)), -0.2, 0.2), 0.0, 1.0)
    east_courant = noise(seeds[2], (LEVELS, NLAT, NLON), 0.3, 1.75, ((0, 4), (1, 8)), jnp.float32)
    north_courant = noise(seeds[3], (LEVELS, NLAT, NLON), 0.3, 1.75, ((0, 4), (1, 8)), jnp.float32)
    vert_courant = noise(seeds[4], (LEVELS, NLAT, NLON), 0.3, 1.75, ((0, 4), (1, 8)), jnp.float32)
    filter_flags = draw_filter_flags(jax.random.fold_in(seeds[7], 71), 0)
    owner_slots = draw_owner_slots(jax.random.fold_in(seeds[7], 71), 0)
    return {"thickness": thickness, "tracers": tracers, "east_courant": east_courant, "north_courant": north_courant, "vert_courant": vert_courant, "filter_flags": filter_flags, "owner_slots": owner_slots}


PI = math.pi
COS_CUT = math.cos(40.0 * math.pi / 180.0)

def spectral_table(nlon):
    column_ids = jnp.arange(nlon, dtype=jnp.int32)
    nyquist = nlon // 2
    wave_num = jnp.where(column_ids <= nyquist, column_ids, column_ids - nyquist)
    angles = (column_ids[:, None] * wave_num[None, :] % nlon).astype(jnp.float32) * (2.0 * PI / nlon)
    weights = jnp.where((column_ids == 0) | (column_ids == nyquist), math.sqrt(1.0 / nlon), math.sqrt(2.0 / nlon)).astype(jnp.float32)
    return jnp.where(column_ids[None, :] <= nyquist, jnp.cos(angles), jnp.sin(angles)) * weights[None, :]

def damping(cos_ratio, nlon):
    column_ids = jnp.arange(nlon, dtype=jnp.int32)
    nyquist = nlon // 2
    wave_num = jnp.where(column_ids <= nyquist, column_ids, column_ids - nyquist)
    sine_wave = jnp.abs(jnp.sin(wave_num.astype(jnp.float32) * (PI / nlon)))
    fraction = cos_ratio[:, None] / jnp.maximum(cos_ratio[:, None], sine_wave[None, :])
    return fraction * fraction

def cell_cosine(row_ids, total_rows):
    return jnp.cos((row_ids.astype(jnp.float32) + 0.5) * (PI / total_rows) - 0.5 * PI)

def face_cosine(row_ids, total_rows):
    return jnp.sin((row_ids + 1).astype(jnp.float32) * (PI / total_rows)) * (row_ids + 1 < total_rows).astype(jnp.float32)

def upwind(courant, first, second):
    return jnp.maximum(courant, 0.0) * first + jnp.minimum(courant, 0.0) * second

def tendency(fields_all, east_courant, north_courant, vert_courant):
    total_levels = fields_all.shape[1]
    total_rows = fields_all.shape[2]
    east_flux = upwind(east_courant, fields_all, jnp.roll(fields_all, -1, axis=3))
    div_east = east_flux - jnp.roll(east_flux, 1, axis=3)
    row_ids = jnp.arange(total_rows, dtype=jnp.int32)
    zero_row = jnp.zeros_like(fields_all[:, :, :1])
    north_next = jnp.concatenate([fields_all[:, :, 1:], zero_row], axis=2)
    north_flux = upwind(north_courant, fields_all, north_next) * face_cosine(row_ids, total_rows)[:, None]
    north_prev = jnp.concatenate([zero_row, north_flux[:, :, :-1]], axis=2)
    div_north = (north_flux - north_prev) / cell_cosine(row_ids, total_rows)[:, None]
    level_ids = jnp.arange(total_levels, dtype=jnp.int32)
    zero_level = jnp.zeros_like(fields_all[:, :1])
    below = jnp.concatenate([fields_all[:, 1:], zero_level], axis=1)
    level_mask = (level_ids + 1 < total_levels).astype(jnp.float32)
    vert_flux = upwind(vert_courant, fields_all, below) * level_mask[:, None, None]
    vert_prev = jnp.concatenate([zero_level, vert_flux[:, :-1]], axis=1)
    div_vert = vert_flux - vert_prev
    return -(div_east + div_north + div_vert)

def reference(thickness, tracers, east_courant, north_courant, vert_courant, filter_flags, owner_slots):
    fields_all = jnp.concatenate([thickness[None], thickness[None] * tracers], axis=0)
    change = tendency(fields_all, east_courant, north_courant, vert_courant)
    row_ids = jnp.arange(NLAT, dtype=jnp.int32)
    target = jnp.where(filter_flags == 1, owner_slots, FILTER_ROWS).astype(jnp.int32)
    slot_rows = jnp.zeros((FILTER_ROWS,), jnp.int32).at[target].set(row_ids, mode='drop')
    dft_table = spectral_table(NLON)
    damping_rows = damping(cell_cosine(slot_rows, NLAT) / COS_CUT, NLON)

    def filter_field(field_change):
        chosen = field_change[:, slot_rows, :]
        coeffs = jnp.einsum('lri,ic->lrc', chosen, dft_table, precision=lax.Precision.HIGHEST) * damping_rows[None]
        restored = jnp.einsum('lrc,ic->lri', coeffs, dft_table, precision=lax.Precision.HIGHEST)
        return (field_change.at[:, slot_rows, :].set(restored), coeffs)
    filtered, coeffs = lax.map(filter_field, change)
    updated = fields_all + filtered
    return (updated[0], updated[1:], jnp.transpose(coeffs[0], (1, 0, 2)))
```

```python
import math

import jax
import jax.numpy as jnp
import numpy as np
from jax import lax
from jax.sharding import PartitionSpec as P

PI = math.pi
COS_CUT = math.cos(40.0 * math.pi / 180.0)


def spectral_table(nlon):
    ids = np.arange(nlon)
    nyquist = nlon // 2
    wave = np.where(ids <= nyquist, ids, ids - nyquist)
    angles = (ids[:, None] * wave[None, :] % nlon) * (2.0 * PI / nlon)
    weights = np.where((ids == 0) | (ids == nyquist), math.sqrt(1.0 / nlon), math.sqrt(2.0 / nlon))
    return np.where(ids[None, :] <= nyquist, np.cos(angles), np.sin(angles)) * weights[None, :]


def sine_wave(nlon):
    ids = np.arange(nlon)
    nyquist = nlon // 2
    wave = np.where(ids <= nyquist, ids, ids - nyquist)
    return np.abs(np.sin(wave * (PI / nlon))).astype(np.float32)


def cell_cosine(row_ids, total_rows):
    return jnp.cos((row_ids.astype(jnp.float32) + 0.5) * (PI / total_rows) - 0.5 * PI)


def face_cosine(row_ids, total_rows):
    return jnp.sin((row_ids + 1).astype(jnp.float32) * (PI / total_rows)) * (
        row_ids + 1 < total_rows
    ).astype(jnp.float32)


def upwind(courant, first, second):
    return jnp.maximum(courant, 0.0) * first + jnp.minimum(courant, 0.0) * second


def split(x):
    hi = lax.reduce_precision(x, 8, 7)
    lo = lax.reduce_precision(x - hi, 8, 7)
    return hi.astype(jnp.bfloat16), lo.astype(jnp.bfloat16)


def product(x, hi, lo, contract):
    dims = (((x.ndim - 1,), (contract,)), ((), ()))
    xh, xl = split(x)
    dot = lambda a, b: lax.dot_general(a, b, dims, preferred_element_type=jnp.float32)
    return dot(xh, hi) + (dot(xl, hi) + dot(xh, lo))


def shifted(x, axis, up):
    count = lax.axis_size(axis)
    pairs = [(i, i + 1) if up else (i + 1, i) for i in range(count - 1)]
    return lax.ppermute(x, axis, pairs)


def spectra_maps(filter_flags, owner_slots, my_band, lat_dev, lat_count, slot_dev):
    total_rows = filter_flags.shape[0]
    cap = -(-lat_dev // lat_count)
    flagged = filter_flags == 1
    owner = jnp.where(flagged, owner_slots // slot_dev, -1)
    place = jnp.where(flagged, owner_slots % slot_dev, 0)
    rows = jnp.arange(total_rows, dtype=jnp.int32)
    source = rows // lat_dev
    earlier = (
        (source[:, None] == source[None, :])
        & (owner[:, None] == owner[None, :])
        & (rows[None, :] < rows[:, None])
    )
    rank = jnp.sum(earlier.astype(jnp.int32), axis=1)
    buffer = jnp.arange(lat_count * cap, dtype=jnp.int32)
    sends = (
        (source[None, :] == my_band)
        & flagged[None, :]
        & ((owner * cap + rank)[None, :] == buffer[:, None])
    )
    pick = jnp.sum(jnp.where(sends, (rows % lat_dev)[None, :], 0), axis=1)
    slots = jnp.arange(slot_dev, dtype=jnp.int32)
    takes = flagged[None, :] & (owner[None, :] == my_band) & (place[None, :] == slots[:, None])
    collect = jnp.sum(jnp.where(takes, (source * cap + rank)[None, :], 0), axis=1)
    return pick, collect


def local(thickness, tracers, east_courant, north_courant, vert_courant, filter_flags, owner_slots, hi, lo):
    lev_dev, lat_dev, nlon = thickness.shape
    lat_count = lax.axis_size("lat")
    lev_count = lax.axis_size("lev")
    slot_dev = 9
    my_band = lax.axis_index("lat")
    my_levels = lax.axis_index("lev")
    total_rows = lat_dev * lat_count
    total_levels = lev_dev * lev_count
    fields = jnp.concatenate([thickness[None], thickness[None] * tracers], axis=0)
    row_last = jnp.concatenate([fields[:, :, -1:], north_courant[None, :, -1:]], axis=0)
    lev_last = jnp.concatenate([fields[:, -1:], vert_courant[None, -1:]], axis=0)
    from_south = shifted(row_last, "lat", True)
    from_north = shifted(fields[:, :, :1], "lat", False)
    from_above = shifted(lev_last, "lev", True)
    from_below = shifted(fields[:, :1], "lev", False)
    rows = my_band * lat_dev + jnp.arange(lat_dev, dtype=jnp.int32)
    levels = my_levels * lev_dev + jnp.arange(lev_dev, dtype=jnp.int32)
    east_flux = upwind(east_courant, fields, jnp.roll(fields, -1, axis=3))
    div_east = east_flux - jnp.roll(east_flux, 1, axis=3)
    x_north = jnp.concatenate([fields[:, :, 1:], from_north], axis=2)
    x_south = jnp.concatenate([from_south[:-1], fields[:, :, :-1]], axis=2)
    south_courant = jnp.concatenate([from_south[-1], north_courant[:, :-1]], axis=1)
    north_flux = upwind(north_courant, fields, x_north) * face_cosine(rows, total_rows)[:, None]
    north_prev = upwind(south_courant, x_south, fields) * face_cosine(rows - 1, total_rows)[:, None]
    div_north = (north_flux - north_prev) / cell_cosine(rows, total_rows)[:, None]
    x_below = jnp.concatenate([fields[:, 1:], from_below], axis=1)
    x_above = jnp.concatenate([from_above[:-1], fields[:, :-1]], axis=1)
    above_courant = jnp.concatenate([from_above[-1], vert_courant[:-1]], axis=0)
    mask = (levels + 1 < total_levels).astype(jnp.float32)[:, None, None]
    div_vert = upwind(vert_courant, fields, x_below) * mask - upwind(above_courant, x_above, fields)
    change = -(div_east + div_north + div_vert)
    ratio = (cell_cosine(rows, total_rows) / COS_CUT)[:, None]
    fraction = ratio / jnp.maximum(ratio, jnp.asarray(sine_wave(nlon))[None, :])
    coeffs = product(change, hi, lo, 0) * (fraction * fraction)
    restored = product(coeffs, hi, lo, 1)
    flags = lax.dynamic_slice_in_dim(filter_flags, my_band * lat_dev, lat_dev) == 1
    updated = fields + jnp.where(flags[None, None, :, None], restored, change)
    pick, collect = spectra_maps(filter_flags, owner_slots, my_band, lat_dev, lat_count, slot_dev)
    outgoing = jnp.take(coeffs[0], pick, axis=1).transpose(1, 0, 2)
    arrived = lax.all_to_all(outgoing, "lat", split_axis=0, concat_axis=0, tiled=True)
    spectra = jnp.take(arrived, collect, axis=0)
    return (updated[0], updated[1:], spectra)


def solution(mesh):
    def run(thickness, tracers, east_courant, north_courant, vert_courant, filter_flags, owner_slots):
        table = spectral_table(thickness.shape[-1]).astype(np.float32)
        high = table.astype(jnp.bfloat16)
        low = (table - high.astype(np.float32)).astype(jnp.bfloat16)
        mapped = jax.shard_map(
            local,
            mesh=mesh,
            in_specs=(
                P("lev", "lat", None),
                P(None, "lev", "lat", None),
                P("lev", "lat", None),
                P("lev", "lat", None),
                P("lev", "lat", None),
                P(),
                P(),
                P(),
                P(),
            ),
            out_specs=(P("lev", "lat", None), P(None, "lev", "lat", None), P("lat", "lev", None)),
            check_vma=False,
        )
        return mapped(
            thickness,
            tracers,
            east_courant,
            north_courant,
            vert_courant,
            filter_flags,
            owner_slots,
            jnp.asarray(high),
            jnp.asarray(low),
        )

    return run
```

```python
import functools
import math

import jax
import jax.numpy as jnp
import numpy as np
from jax import lax
from jax.experimental import pallas as pl
from jax.experimental.pallas import tpu as pltpu
from jax.sharding import PartitionSpec as P

SLOT_DEV = 9
CHUNK = 256
PI = math.pi
COS_CUT = math.cos(40.0 * math.pi / 180.0)
F32 = jnp.float32
BF16 = jnp.bfloat16


def wave_numbers(nlon):
    ids = np.arange(nlon)
    return ids, np.where(ids <= nlon // 2, ids, ids - nlon // 2)


def spectral_table(nlon, padded):
    ids, wave = wave_numbers(nlon)
    angles = (ids[:, None] * wave[None, :] % nlon) * (2.0 * PI / nlon)
    edge = (ids == 0) | (ids == nlon // 2)
    weights = np.where(edge, math.sqrt(1.0 / nlon), math.sqrt(2.0 / nlon))
    table = np.where(ids[None, :] <= nlon // 2, np.cos(angles), np.sin(angles)) * weights[None, :]
    full = np.zeros((padded, padded), np.float32)
    full[:nlon, :nlon] = table
    high = full.astype(BF16)
    low = (full - high.astype(np.float32)).astype(BF16)
    return high, low


def sine_rows(nlon, padded):
    sines = np.ones((8, padded), np.float32)
    sines[:, :nlon] = np.abs(np.sin(wave_numbers(nlon)[1] * (PI / nlon)))
    return sines


def row_constants(total_rows):
    rows = np.arange(total_rows)
    cosine = np.cos((rows + 0.5) * (PI / total_rows) - 0.5 * PI)
    face = np.where(rows + 1 < total_rows, np.sin((rows + 1) * (PI / total_rows)), 0.0)
    before = np.where(rows > 0, np.sin(rows * (PI / total_rows)), 0.0)
    out = np.zeros((total_rows, 128), np.float32)
    out[:, 0] = cosine / COS_CUT
    out[:, 1] = face / cosine
    out[:, 2] = before / cosine
    return out


def next_lane(x):
    return jnp.concatenate([x[:, 1:], x[:, :1]], axis=1)


def prev_lane(x):
    return jnp.concatenate([x[:, -1:], x[:, :-1]], axis=1)


def pos(x):
    return jnp.maximum(x, 0.0)


def neg(x):
    return jnp.minimum(x, 0.0)


def kernel(
    lat_count, lev_count, cap,
    th_in, tr_in, east_in, north_in, vert_in, flags, slots, slots_row, high_in, low_in, rowc_in, sines,
    th_out, tr_out, spectra,
    th, tr, vert, east, north, high, low, rowc,
    up_buf, down_buf, from_south, from_north,
    damp, change, left, mid, res, coef0, packed, arrived, out_buf,
    in_sems, lev_send, lev_recv, lat_send, lat_recv, sp_send, sp_recv, self_sems, out_sems,
):
    fields = tr_in.shape[0] + 1
    rows_dev, nlon = th_in.shape[1], th_in.shape[2]
    padded = high.shape[0]
    count = fields * rows_dev
    band = lax.axis_index("lat")
    lev = lax.axis_index("lev")

    loads = [
        pltpu.make_async_copy(th_in, th.at[pl.ds(1, 2)], in_sems.at[0]),
        pltpu.make_async_copy(tr_in, tr.at[:, pl.ds(1, 2)], in_sems.at[1]),
        pltpu.make_async_copy(north_in, north, in_sems.at[2]),
        pltpu.make_async_copy(vert_in, vert.at[pl.ds(1, 2)], in_sems.at[3]),
        pltpu.make_async_copy(east_in, east, in_sems.at[4]),
        pltpu.make_async_copy(rowc_in.at[pl.ds(band * rows_dev, rows_dev)], rowc, in_sems.at[5]),
        pltpu.make_async_copy(high_in, high, in_sems.at[6]),
        pltpu.make_async_copy(low_in, low, in_sems.at[7]),
    ]
    for load in loads[:6]:
        load.start()

    barrier = pltpu.get_barrier_semaphore()

    def greet(peer):
        pl.semaphore_signal(barrier, inc=1, device_id=peer, device_id_type=pl.DeviceIdType.MESH)

    for k in range(1, lat_count):
        greet((lax.rem(band + k, lat_count), lev))

    @pl.when(lev > 0)
    def _():
        greet((band, lev - 1))

    @pl.when(lev < lev_count - 1)
    def _():
        greet((band, lev + 1))

    beside = jnp.where(lev > 0, 1, 0) + jnp.where(lev < lev_count - 1, 1, 0)
    pl.semaphore_wait(barrier, lat_count - 1 + beside)

    def remote(src, dst, send, recv, peer):
        return pltpu.make_async_remote_copy(
            src_ref=src, dst_ref=dst, send_sem=send, recv_sem=recv,
            device_id=peer, device_id_type=pl.DeviceIdType.MESH,
        )

    down = (band, lev + 1)
    up = (band, lev - 1)
    to_next = [
        remote(th_in.at[1], th.at[0], lev_send.at[0], lev_recv.at[0], down),
        remote(vert_in.at[1], vert.at[0], lev_send.at[1], lev_recv.at[1], down),
        remote(tr_in.at[:, 1], tr.at[:, 0], lev_send.at[2], lev_recv.at[2], down),
    ]
    to_prev = [
        remote(th_in.at[0], th.at[3], lev_send.at[3], lev_recv.at[3], up),
        remote(tr_in.at[:, 0], tr.at[:, 3], lev_send.at[4], lev_recv.at[4], up),
    ]

    @pl.when(lev < lev_count - 1)
    def _():
        for copy in to_next:
            copy.start()

    @pl.when(lev > 0)
    def _():
        for copy in to_prev:
            copy.start()

    for load in loads[6:]:
        load.start()

    @pl.when(lev == 0)
    def _():
        th[0] = jnp.zeros_like(th[0])
        vert[0] = jnp.zeros_like(vert[0])
        tr[:, 0] = jnp.zeros_like(tr[:, 0])

    @pl.when(lev == lev_count - 1)
    def _():
        th[3] = jnp.zeros_like(th[3])
        tr[:, 3] = jnp.zeros_like(tr[:, 3])

    for load in loads[:3]:
        load.wait()
    up_buf[...] = jnp.zeros_like(up_buf)
    down_buf[...] = jnp.zeros_like(down_buf)
    for l in range(2):
        for buf, at in ((up_buf, rows_dev - 1), (down_buf, 0)):
            base = th[l + 1, at : at + 1, :]
            buf[l, 0:1, :] = base
            for f in range(1, fields):
                buf[l, f : f + 1, :] = base * tr[f - 1, l + 1, at : at + 1, :]
        up_buf[l, fields : fields + 1, :] = north[l, rows_dev - 1 : rows_dev, :]
    to_north = remote(up_buf, from_south, lat_send.at[0], lat_recv.at[0], (band + 1, lev))
    to_south = remote(down_buf, from_north, lat_send.at[1], lat_recv.at[1], (band - 1, lev))

    @pl.when(band < lat_count - 1)
    def _():
        to_north.start()

    @pl.when(band > 0)
    def _():
        to_south.start()

    @pl.when(band == 0)
    def _():
        from_south[...] = jnp.zeros_like(from_south)

    @pl.when(band == lat_count - 1)
    def _():
        from_north[...] = jnp.zeros_like(from_north)

    for load in loads[3:6]:
        load.wait()
    ratio = rowc[:, 0:1]
    fraction = ratio / jnp.maximum(ratio, sines[0:1, :])
    damp[...] = fraction * fraction
    left[:, nlon:] = jnp.zeros((2 * count, padded - nlon), BF16)

    row_iota = lax.broadcasted_iota(jnp.int32, (rows_dev, 1), 0)
    owners, keys = [], []
    flag_col = jnp.zeros((rows_dev, 1), jnp.int32)
    for j in range(rows_dev):
        flag = flags[band * rows_dev + j]
        slot = slots[band * rows_dev + j]
        owner = jnp.where((flag == 1) & (slot >= 0), lax.div(jnp.maximum(slot, 0), SLOT_DEV), -1)
        rank = jnp.int32(0)
        for other in owners:
            rank = rank + jnp.where(other == owner, 1, 0)
        owners.append(owner)
        keys.append(jnp.where(owner >= 0, owner * cap + rank, -1))
        flag_col = jnp.where(row_iota == j, flag, flag_col)
    flagged = flag_col == 1
    picks = []
    for q in range(lat_count * cap):
        pick = jnp.int32(0)
        for j in range(rows_dev):
            pick = jnp.where(keys[j] == q, j, pick)
        picks.append(pick)

    row = slots_row[...]
    total = row.shape[1]
    slot_rows = 16
    lane = lax.broadcasted_iota(jnp.int32, (slot_rows, total), 1)
    place = lax.broadcasted_iota(jnp.int32, (slot_rows, total), 0)
    first = band * SLOT_DEV
    shift = rows_dev.bit_length() - 1
    full = jnp.broadcast_to(row, (slot_rows, total))
    hit = (full == first + place) & (place < SLOT_DEV)
    source_row = jnp.sum(jnp.where(hit, lane, 0).astype(F32), axis=1, keepdims=True).astype(jnp.int32)
    source = lax.shift_right_logical(source_row, shift)
    mine = (full >= first) & (full < first + SLOT_DEV)
    before = mine & (lax.shift_right_logical(lane, shift) == source) & (lane < source_row)
    ranks = jnp.sum(jnp.where(before, 1.0, 0.0), axis=1, keepdims=True).astype(jnp.int32)
    arrival = source * cap + ranks

    @pl.when(band < lat_count - 1)
    def _():
        to_south.wait_recv()

    @pl.when(band > 0)
    def _():
        to_north.wait_recv()

    def spectra_copy(l, k):
        peer = lax.rem(band + k, lat_count)
        return remote(
            packed.at[l, peer], arrived.at[l, band], sp_send.at[l, peer], sp_recv.at[l, band], (peer, lev)
        )

    def spectra_arrival(l, k):
        peer = lax.rem(band + k, lat_count)
        return remote(
            packed.at[l, peer], arrived.at[l, peer], sp_send.at[l, peer], sp_recv.at[l, peer], (peer, lev)
        )

    def own_copy(l):
        return pltpu.make_async_copy(packed.at[l, band], arrived.at[l, band], self_sems.at[l])

    def out_copies(l):
        return [
            pltpu.make_async_copy(out_buf.at[l, 0], th_out.at[l], out_sems.at[l, 0]),
            pltpu.make_async_copy(out_buf.at[l, pl.ds(1, fields - 1)], tr_out.at[:, l], out_sems.at[l, 1]),
        ]

    def product(ref, table, at, across):
        part = pl.ds(at * CHUNK, CHUNK)
        dims = (((1,), (1,)), ((), ())) if across else (((1,), (0,)), ((), ()))
        pick = (lambda t: t[part, :]) if across else (lambda t: t[:, part])
        both = lax.dot_general(ref[...], pick(high), dims, preferred_element_type=F32)
        rest = lax.dot_general(ref[0:count, :], pick(low), dims, preferred_element_type=F32)
        return both[:count] + (both[count:] + rest)

    def split_to(ref, at, cols, x):
        n = x.shape[0]
        hi = x.astype(BF16)
        ref[at : at + n, cols] = hi
        ref[count + at : count + at + n, cols] = (x - hi.astype(F32)).astype(BF16)

    def level(t, carry):
        even = lax.rem(lev, 2)
        l = jnp.where(t == 0, 1 - even, even)

        @pl.when((l == 0) & (lev > 0))
        def _():
            for copy in to_next:
                copy.wait_recv()

        @pl.when((l == 1) & (lev < lev_count - 1))
        def _():
            for copy in to_prev:
                copy.wait_recv()

        inner = jnp.where(lev * 2 + l + 1 < lev_count * 2, 1.0, 0.0).astype(F32)
        e = east[l]
        ew = prev_lane(e)
        n = north[l]
        ns = jnp.concatenate([from_south[l, fields : fields + 1, :], n[:-1, :]], axis=0)
        v = vert[l + 1] * inner
        va = vert[l]
        fn = rowc[:, 1:2]
        fs = rowc[:, 2:3]
        centre = pos(e) - neg(ew) + fn * pos(n) - fs * neg(ns) + (pos(v) - neg(va))
        c_e, c_w = neg(e), pos(ew)
        c_n, c_s = fn * neg(n), fs * pos(ns)
        c_b, c_a = neg(v), pos(va)
        for f in range(fields):
            if f == 0:
                x, above, below = th[l + 1], th[l], th[l + 2]
            else:
                x = th[l + 1] * tr[f - 1, l + 1]
                above = th[l] * tr[f - 1, l]
                below = th[l + 2] * tr[f - 1, l + 2]
            x_n = jnp.concatenate([x[1:, :], from_north[l, f : f + 1, :]], axis=0)
            x_s = jnp.concatenate([from_south[l, f : f + 1, :], x[:-1, :]], axis=0)
            tend = (c_w * prev_lane(x) - c_e * next_lane(x)) + (c_s * x_s - c_n * x_n)
            tend = tend + (c_a * above - c_b * below) - centre * x
            change[f * rows_dev : (f + 1) * rows_dev, :] = tend
            out_buf[l, f] = x
            split_to(left, f * rows_dev, slice(0, nlon), tend)

        @pl.when(t == 0)
        def _():
            for load in loads[6:]:
                load.wait()

        for at in range(padded // CHUNK):
            cols = slice(at * CHUNK, (at + 1) * CHUNK)
            coef = product(left, high, at, False).reshape(fields, rows_dev, CHUNK)
            coef = (coef * damp[:, cols][None]).reshape(count, CHUNK)
            coef0[:, cols] = coef[:rows_dev]
            split_to(mid, 0, cols, coef)
        for q in range(lat_count * cap):
            packed[l, q // cap, q % cap : q % cap + 1, :] = coef0[pl.ds(picks[q], 1), :][:, :nlon]
        own_copy(l).start()
        for k in range(1, lat_count):
            spectra_copy(l, k).start()
        for at in range(padded // CHUNK):
            cols = slice(at * CHUNK, (at + 1) * CHUNK)
            res[:, cols] = product(mid, high, at, True)
        for f in range(fields):
            part = slice(f * rows_dev, (f + 1) * rows_dev)
            out_buf[l, f] = out_buf[l, f] + jnp.where(flagged, res[part, :nlon], change[part, :])
        for copy in out_copies(l):
            copy.start()
        return carry

    lax.fori_loop(0, 2, level, 0)

    for l in range(2):
        own_copy(l).wait()
        for k in range(1, lat_count):
            spectra_arrival(l, k).wait_recv()
        value = jnp.zeros((slot_rows, nlon), F32)
        for q in range(lat_count * cap):
            value = jnp.where(arrival == q, arrived[l, q // cap, q % cap : q % cap + 1, :], value)
        for p in range(SLOT_DEV):
            spectra[p, l : l + 1, :] = value[p : p + 1, :]
        for k in range(1, lat_count):
            spectra_copy(l, k).wait_send()

    @pl.when(lev < lev_count - 1)
    def _():
        for copy in to_next:
            copy.wait_send()

    @pl.when(lev > 0)
    def _():
        for copy in to_prev:
            copy.wait_send()

    @pl.when(band < lat_count - 1)
    def _():
        to_north.wait_send()

    @pl.when(band > 0)
    def _():
        to_south.wait_send()

    for l in range(2):
        for copy in out_copies(l):
            copy.wait()


def local(thickness, tracers, east, north, vert, flags, slots, high, low, rowc, sines):
    lat_count = lax.axis_size("lat")
    lev_count = lax.axis_size("lev")
    lev_dev, rows_dev, nlon = thickness.shape
    padded = high.shape[0]
    fields = tracers.shape[0] + 1
    count = fields * rows_dev
    cap = -(-rows_dev // lat_count)
    anywhere = pl.BlockSpec(memory_space=pl.ANY)
    vmem = pl.BlockSpec(memory_space=pltpu.VMEM)
    smem = pl.BlockSpec(memory_space=pltpu.SMEM)
    dma = pltpu.SemaphoreType.DMA
    return pl.pallas_call(
        functools.partial(kernel, lat_count, lev_count, cap),
        out_shape=(
            jax.ShapeDtypeStruct(thickness.shape, F32),
            jax.ShapeDtypeStruct(tracers.shape, F32),
            jax.ShapeDtypeStruct((SLOT_DEV, lev_dev, nlon), F32),
        ),
        in_specs=[anywhere] * 5 + [smem, smem, vmem] + [anywhere] * 3 + [vmem],
        out_specs=(anywhere, anywhere, vmem),
        scratch_shapes=[
            pltpu.VMEM((4, rows_dev, nlon), F32),
            pltpu.VMEM((fields - 1, 4, rows_dev, nlon), F32),
            pltpu.VMEM((3, rows_dev, nlon), F32),
            pltpu.VMEM((2, rows_dev, nlon), F32),
            pltpu.VMEM((2, rows_dev, nlon), F32),
            pltpu.VMEM((padded, padded), BF16),
            pltpu.VMEM((padded, padded), BF16),
            pltpu.VMEM((rows_dev, 128), F32),
            pltpu.VMEM((2, 16, nlon), F32),
            pltpu.VMEM((2, 16, nlon), F32),
            pltpu.VMEM((2, 16, nlon), F32),
            pltpu.VMEM((2, 16, nlon), F32),
            pltpu.VMEM((rows_dev, padded), F32),
            pltpu.VMEM((count, nlon), F32),
            pltpu.VMEM((2 * count, padded), BF16),
            pltpu.VMEM((2 * count, padded), BF16),
            pltpu.VMEM((count, padded), F32),
            pltpu.VMEM((rows_dev, padded), F32),
            pltpu.VMEM((2, lat_count, cap, nlon), F32),
            pltpu.VMEM((2, lat_count, cap, nlon), F32),
            pltpu.VMEM((2, fields, rows_dev, nlon), F32),
            dma((8,)),
            dma((5,)),
            dma((5,)),
            dma((2,)),
            dma((2,)),
            dma((2, lat_count)),
            dma((2, lat_count)),
            dma((2,)),
            dma((2, 2)),
        ],
        compiler_params=pltpu.CompilerParams(
            collective_id=0, has_side_effects=True, vmem_limit_bytes=48 * 1024 * 1024
        ),
    )(thickness, tracers, east, north, vert, flags, slots, slots.reshape(1, -1), high, low, rowc, sines)


def solution(mesh):
    def run(thickness, tracers, east, north, vert, flags, slots):
        total_rows, nlon = thickness.shape[1:]
        padded = -(-nlon // CHUNK) * CHUNK
        high, low = spectral_table(nlon, padded)
        cells = P("lev", "lat", None)
        mapped = jax.shard_map(
            local,
            mesh=mesh,
            in_specs=(cells, P(None, "lev", "lat", None), cells, cells, cells) + (P(),) * 6,
            out_specs=(cells, P(None, "lev", "lat", None), P("lat", "lev", None)),
            check_vma=False,
        )
        tables = (high, low, row_constants(total_rows), sine_rows(nlon, padded))
        return mapped(
            thickness, tracers, east, north, vert, flags, slots, *(jnp.asarray(t) for t in tables)
        )

    return run
```

```python
import functools
import math

import jax
import jax.numpy as jnp
import numpy as np
from jax import lax
from jax.experimental import pallas as pl
from jax.experimental.pallas import tpu as pltpu
from jax.sharding import PartitionSpec as P

SLOT_DEV = 9
CHUNK = 256
PI = math.pi
COS_CUT = math.cos(40.0 * math.pi / 180.0)
F32 = jnp.float32
BF16 = jnp.bfloat16


def columns(nlon):
    half, quarter = nlon // 2, nlon // 4
    part = -(-(quarter + 1) // 128) * 128
    waves = np.full((2, 2, part), -1)
    waves[0, 0, : quarter + 1] = 2 * np.arange(quarter + 1)
    waves[0, 1, 1:quarter] = 2 * np.arange(1, quarter)
    waves[1, :, :quarter] = 2 * np.arange(quarter) + 1
    return half, part, waves


def spectral_table(nlon):
    half, part, waves = columns(nlon)
    full = np.zeros((2, 2 * part, 2, part), np.float32)
    angles = (np.arange(half)[:, None, None, None] * waves[None] % nlon) * (2.0 * PI / nlon)
    edge = (waves == 0) | (waves == half)
    weights = np.where(edge, math.sqrt(1.0 / nlon), math.sqrt(2.0 / nlon)) * (waves >= 0)
    table = np.stack([np.cos(angles[:, :, 0]), np.sin(angles[:, :, 1])], axis=2) * weights[None]
    full[:, :half] = np.moveaxis(table, 1, 0)
    full = full.reshape(2, 2 * part, 2 * part)
    high = full.astype(BF16)
    low = (full - high.astype(np.float32)).astype(BF16)
    return high, low


def sine_rows(nlon):
    _, _, waves = columns(nlon)
    sines = np.where(waves >= 0, np.abs(np.sin(waves * (PI / nlon))), 1.0).reshape(1, -1)
    return np.broadcast_to(sines, (8, sines.shape[1])).astype(np.float32)


def interleave():
    out = np.zeros((CHUNK, CHUNK), np.float32)
    ids = np.arange(CHUNK // 2)
    out[ids, 2 * ids] = 1.0
    out[CHUNK // 2 + ids, 2 * ids + 1] = 1.0
    return out.astype(BF16)


def row_constants(total_rows):
    rows = np.arange(total_rows)
    cosine = np.cos((rows + 0.5) * (PI / total_rows) - 0.5 * PI)
    face = np.where(rows + 1 < total_rows, np.sin((rows + 1) * (PI / total_rows)), 0.0)
    before = np.where(rows > 0, np.sin(rows * (PI / total_rows)), 0.0)
    out = np.zeros((total_rows, 128), np.float32)
    out[:, 0] = cosine / COS_CUT
    out[:, 1] = face / cosine
    out[:, 2] = before / cosine
    return out


def next_lane(x):
    return jnp.concatenate([x[:, 1:], x[:, :1]], axis=1)


def prev_lane(x):
    return jnp.concatenate([x[:, -1:], x[:, :-1]], axis=1)


def pos(x):
    return jnp.maximum(x, 0.0)


def neg(x):
    return jnp.minimum(x, 0.0)


def kernel(
    lat_count, lev_count, cap,
    th_in, tr_in, east_in, north_in, vert_in, flags_in, slots_in, row_in, high_in, low_in, rowc_in, sines_in, weave_in,
    th_out, tr_out, spectra,
    th, tr, vert, east, north, high, low, rowc, sines, weave, slots_row, flags, slots,
    up_buf, down_buf, from_south, from_north,
    damp, change, left, mid, res, coef0, packed, arrived, out_buf,
    in_sems, lev_send, lev_recv, lat_send, lat_recv, sp_send, sp_recv, self_sems, out_sems,
):
    fields = tr_in.shape[0] + 1
    rows_dev, nlon = th_in.shape[1], th_in.shape[2]
    half, padded = nlon // 2, high.shape[1]
    count = fields * rows_dev
    band = lax.axis_index("lat")
    lev = lax.axis_index("lev")

    loads = [
        pltpu.make_async_copy(th_in, th.at[pl.ds(1, 2)], in_sems.at[0]),
        pltpu.make_async_copy(tr_in, tr.at[:, pl.ds(1, 2)], in_sems.at[1]),
        pltpu.make_async_copy(north_in, north, in_sems.at[2]),
        pltpu.make_async_copy(vert_in, vert.at[pl.ds(1, 2)], in_sems.at[3]),
        pltpu.make_async_copy(east_in, east, in_sems.at[4]),
        pltpu.make_async_copy(rowc_in.at[pl.ds(band * rows_dev, rows_dev)], rowc, in_sems.at[5]),
        pltpu.make_async_copy(sines_in, sines, in_sems.at[6]),
        pltpu.make_async_copy(row_in, slots_row, in_sems.at[7]),
        pltpu.make_async_copy(flags_in, flags, in_sems.at[8]),
        pltpu.make_async_copy(slots_in, slots, in_sems.at[9]),
        pltpu.make_async_copy(high_in, high, in_sems.at[10]),
        pltpu.make_async_copy(low_in, low, in_sems.at[11]),
        pltpu.make_async_copy(weave_in, weave, in_sems.at[12]),
    ]
    for load in loads[:10]:
        load.start()

    barrier = pltpu.get_barrier_semaphore()

    def greet(peer):
        pl.semaphore_signal(barrier, inc=1, device_id=peer, device_id_type=pl.DeviceIdType.MESH)

    for k in range(1, lat_count):
        greet((lax.rem(band + k, lat_count), lev))

    @pl.when(lev > 0)
    def _():
        greet((band, lev - 1))

    @pl.when(lev < lev_count - 1)
    def _():
        greet((band, lev + 1))

    beside = jnp.where(lev > 0, 1, 0) + jnp.where(lev < lev_count - 1, 1, 0)
    pl.semaphore_wait(barrier, lat_count - 1 + beside)

    def remote(src, dst, send, recv, peer):
        return pltpu.make_async_remote_copy(
            src_ref=src, dst_ref=dst, send_sem=send, recv_sem=recv,
            device_id=peer, device_id_type=pl.DeviceIdType.MESH,
        )

    down = (band, lev + 1)
    up = (band, lev - 1)
    to_next = [
        remote(th_in.at[1], th.at[0], lev_send.at[0], lev_recv.at[0], down),
        remote(vert_in.at[1], vert.at[0], lev_send.at[1], lev_recv.at[1], down),
        remote(tr_in.at[:, 1], tr.at[:, 0], lev_send.at[2], lev_recv.at[2], down),
    ]
    to_prev = [
        remote(th_in.at[0], th.at[3], lev_send.at[3], lev_recv.at[3], up),
        remote(tr_in.at[:, 0], tr.at[:, 3], lev_send.at[4], lev_recv.at[4], up),
    ]

    @pl.when(lev < lev_count - 1)
    def _():
        for copy in to_next:
            copy.start()

    @pl.when(lev > 0)
    def _():
        for copy in to_prev:
            copy.start()

    for load in loads[10:]:
        load.start()

    @pl.when(lev == 0)
    def _():
        th[0] = jnp.zeros_like(th[0])
        vert[0] = jnp.zeros_like(vert[0])
        tr[:, 0] = jnp.zeros_like(tr[:, 0])

    @pl.when(lev == lev_count - 1)
    def _():
        th[3] = jnp.zeros_like(th[3])
        tr[:, 3] = jnp.zeros_like(tr[:, 3])

    for load in loads[:3]:
        load.wait()
    up_buf[...] = jnp.zeros_like(up_buf)
    down_buf[...] = jnp.zeros_like(down_buf)
    for l in range(2):
        for buf, at in ((up_buf, rows_dev - 1), (down_buf, 0)):
            base = th[l + 1, at : at + 1, :]
            buf[l, 0:1, :] = base
            for f in range(1, fields):
                buf[l, f : f + 1, :] = base * tr[f - 1, l + 1, at : at + 1, :]
        up_buf[l, fields : fields + 1, :] = north[l, rows_dev - 1 : rows_dev, :]
    to_north = remote(up_buf, from_south, lat_send.at[0], lat_recv.at[0], (band + 1, lev))
    to_south = remote(down_buf, from_north, lat_send.at[1], lat_recv.at[1], (band - 1, lev))

    @pl.when(band < lat_count - 1)
    def _():
        to_north.start()

    @pl.when(band > 0)
    def _():
        to_south.start()

    @pl.when(band == 0)
    def _():
        from_south[...] = jnp.zeros_like(from_south)

    @pl.when(band == lat_count - 1)
    def _():
        from_north[...] = jnp.zeros_like(from_north)

    for load in loads[3:10]:
        load.wait()
    ratio = rowc[:, 0:1]
    fraction = ratio / jnp.maximum(ratio, sines[0:1, :])
    damp[...] = fraction * fraction
    left[:, :, half:] = jnp.zeros((2, 2 * count, padded - half), BF16)

    row_iota = lax.broadcasted_iota(jnp.int32, (rows_dev, 1), 0)
    owners, keys = [], []
    flag_col = jnp.zeros((rows_dev, 1), jnp.int32)
    for j in range(rows_dev):
        flag = flags[band * rows_dev + j]
        slot = slots[band * rows_dev + j]
        owner = jnp.where((flag == 1) & (slot >= 0), lax.div(jnp.maximum(slot, 0), SLOT_DEV), -1)
        rank = jnp.int32(0)
        for other in owners:
            rank = rank + jnp.where(other == owner, 1, 0)
        owners.append(owner)
        keys.append(jnp.where(owner >= 0, owner * cap + rank, -1))
        flag_col = jnp.where(row_iota == j, flag, flag_col)
    flagged = flag_col == 1
    picks = []
    for q in range(lat_count * cap):
        pick = jnp.int32(0)
        for j in range(rows_dev):
            pick = jnp.where(keys[j] == q, j, pick)
        picks.append(pick)

    row = slots_row[...]
    total = row.shape[1]
    slot_rows = 16
    lane = lax.broadcasted_iota(jnp.int32, (slot_rows, total), 1)
    place = lax.broadcasted_iota(jnp.int32, (slot_rows, total), 0)
    first = band * SLOT_DEV
    shift = rows_dev.bit_length() - 1
    full = jnp.broadcast_to(row, (slot_rows, total))
    hit = (full == first + place) & (place < SLOT_DEV)
    source_row = jnp.sum(jnp.where(hit, lane, 0).astype(F32), axis=1, keepdims=True).astype(jnp.int32)
    source = lax.shift_right_logical(source_row, shift)
    mine = (full >= first) & (full < first + SLOT_DEV)
    before = mine & (lax.shift_right_logical(lane, shift) == source) & (lane < source_row)
    ranks = jnp.sum(jnp.where(before, 1.0, 0.0), axis=1, keepdims=True).astype(jnp.int32)
    arrival = source * cap + ranks

    @pl.when(band < lat_count - 1)
    def _():
        to_south.wait_recv()

    @pl.when(band > 0)
    def _():
        to_north.wait_recv()

    def spectra_copy(l, k):
        peer = lax.rem(band + k, lat_count)
        return remote(
            packed.at[l, peer], arrived.at[l, band], sp_send.at[l, peer], sp_recv.at[l, band], (peer, lev)
        )

    def spectra_arrival(l, k):
        peer = lax.rem(band + k, lat_count)
        return remote(
            packed.at[l, peer], arrived.at[l, peer], sp_send.at[l, peer], sp_recv.at[l, peer], (peer, lev)
        )

    def own_copy(l):
        return pltpu.make_async_copy(packed.at[l, band], arrived.at[l, band], self_sems.at[l])

    def out_copies(l):
        return [
            pltpu.make_async_copy(out_buf.at[l, 0], th_out.at[l], out_sems.at[l, 0]),
            pltpu.make_async_copy(out_buf.at[l, pl.ds(1, fields - 1)], tr_out.at[:, l], out_sems.at[l, 1]),
        ]

    def product(ref, side, at, across):
        part = pl.ds(at * CHUNK, CHUNK)
        dims = (((1,), (1,)), ((), ())) if across else (((1,), (0,)), ((), ()))
        pick = (lambda t: t[side, part, :]) if across else (lambda t: t[side, :, part])
        both = lax.dot_general(ref[side], pick(high), dims, preferred_element_type=F32)
        rest = lax.dot_general(ref[side, 0:count, :], pick(low), dims, preferred_element_type=F32)
        return both[:count] + (both[count:] + rest)

    def split_to(ref, side, at, cols, x):
        n = x.shape[0]
        hi = x.astype(BF16)
        ref[side, at : at + n, cols] = hi
        ref[side, count + at : count + at + n, cols] = (x - hi.astype(F32)).astype(BF16)

    def level(t, carry):
        even = lax.rem(lev, 2)
        l = jnp.where(t == 0, 1 - even, even)

        @pl.when((l == 0) & (lev > 0))
        def _():
            for copy in to_next:
                copy.wait_recv()

        @pl.when((l == 1) & (lev < lev_count - 1))
        def _():
            for copy in to_prev:
                copy.wait_recv()

        inner = jnp.where(lev * 2 + l + 1 < lev_count * 2, 1.0, 0.0).astype(F32)
        e = east[l]
        ew = prev_lane(e)
        n = north[l]
        ns = jnp.concatenate([from_south[l, fields : fields + 1, :], n[:-1, :]], axis=0)
        v = vert[l + 1] * inner
        va = vert[l]
        fn = rowc[:, 1:2]
        fs = rowc[:, 2:3]
        centre = pos(e) - neg(ew) + fn * pos(n) - fs * neg(ns) + (pos(v) - neg(va))
        c_e, c_w = neg(e), pos(ew)
        c_n, c_s = fn * neg(n), fs * pos(ns)
        c_b, c_a = neg(v), pos(va)
        for f in range(fields):
            if f == 0:
                x, above, below = th[l + 1], th[l], th[l + 2]
            else:
                x = th[l + 1] * tr[f - 1, l + 1]
                above = th[l] * tr[f - 1, l]
                below = th[l + 2] * tr[f - 1, l + 2]
            x_n = jnp.concatenate([x[1:, :], from_north[l, f : f + 1, :]], axis=0)
            x_s = jnp.concatenate([from_south[l, f : f + 1, :], x[:-1, :]], axis=0)
            tend = (c_w * prev_lane(x) - c_e * next_lane(x)) + (c_s * x_s - c_n * x_n)
            tend = tend + (c_a * above - c_b * below) - centre * x
            change[f * rows_dev : (f + 1) * rows_dev, :] = tend
            out_buf[l, f] = x
            split_to(left, 0, f * rows_dev, slice(0, half), tend[:, :half] + tend[:, half:])
            split_to(left, 1, f * rows_dev, slice(0, half), tend[:, :half] - tend[:, half:])

        @pl.when(t == 0)
        def _():
            for load in loads[10:]:
                load.wait()

        for side in range(2):
            for at in range(padded // CHUNK):
                cols = slice(at * CHUNK, (at + 1) * CHUNK)
                coef = product(left, side, at, False).reshape(fields, rows_dev, CHUNK)
                coef = coef * damp[:, side * padded + at * CHUNK : side * padded + (at + 1) * CHUNK][None]
                split_to(mid, side, 0, cols, coef.reshape(count, CHUNK))
        lanes = CHUNK // 2
        rows_of = (slice(0, rows_dev), slice(count, count + rows_dev))
        pieces = []
        for at in range(padded // lanes):
            cols = slice(at * lanes, (at + 1) * lanes)
            pairs = [jnp.concatenate([mid[0, r, cols], mid[1, r, cols]], axis=1) for r in rows_of]
            both = jnp.dot(jnp.concatenate(pairs, axis=0), weave[...], preferred_element_type=F32)
            pieces.append(both[:rows_dev] + both[rows_dev:])
        cosines = jnp.concatenate(pieces[: len(pieces) // 2], axis=1)
        waves = jnp.concatenate(pieces[len(pieces) // 2 :], axis=1)
        coef0[...] = jnp.concatenate([cosines[:, : half + 1], waves[:, 1:half]], axis=1)
        for q in range(lat_count * cap):
            packed[l, q // cap, q % cap : q % cap + 1, :] = coef0[pl.ds(picks[q], 1), :]
        own_copy(l).start()
        for k in range(1, lat_count):
            spectra_copy(l, k).start()
        for side in range(2):
            for at in range(padded // CHUNK):
                res[side, :, at * CHUNK : (at + 1) * CHUNK] = product(mid, side, at, True)
        for f in range(fields):
            part = slice(f * rows_dev, (f + 1) * rows_dev)
            even_part, odd_part = res[0, part, :half], res[1, part, :half]
            filtered = jnp.concatenate([even_part + odd_part, even_part - odd_part], axis=1)
            out_buf[l, f] = out_buf[l, f] + jnp.where(flagged, filtered, change[part, :])
        for copy in out_copies(l):
            copy.start()
        return carry

    lax.fori_loop(0, 2, level, 0)

    for l in range(2):
        own_copy(l).wait()
        for k in range(1, lat_count):
            spectra_arrival(l, k).wait_recv()
        value = jnp.zeros((slot_rows, nlon), F32)
        for q in range(lat_count * cap):
            value = jnp.where(arrival == q, arrived[l, q // cap, q % cap : q % cap + 1, :], value)
        for p in range(SLOT_DEV):
            spectra[p, l : l + 1, :] = value[p : p + 1, :]
        for k in range(1, lat_count):
            spectra_copy(l, k).wait_send()

    @pl.when(lev < lev_count - 1)
    def _():
        for copy in to_next:
            copy.wait_send()

    @pl.when(lev > 0)
    def _():
        for copy in to_prev:
            copy.wait_send()

    @pl.when(band < lat_count - 1)
    def _():
        to_north.wait_send()

    @pl.when(band > 0)
    def _():
        to_south.wait_send()

    for l in range(2):
        for copy in out_copies(l):
            copy.wait()


def local(thickness, tracers, east, north, vert, flags, slots, *tables):
    lat_count = lax.axis_size("lat")
    lev_count = lax.axis_size("lev")
    lev_dev, rows_dev, nlon = thickness.shape
    padded = tables[0].shape[1]
    fields = tracers.shape[0] + 1
    count = fields * rows_dev
    cap = -(-rows_dev // lat_count)
    hbm = pl.BlockSpec(memory_space=pltpu.HBM)
    vmem = pl.BlockSpec(memory_space=pltpu.VMEM)
    dma = pltpu.SemaphoreType.DMA
    return pl.pallas_call(
        functools.partial(kernel, lat_count, lev_count, cap),
        out_shape=(
            jax.ShapeDtypeStruct(thickness.shape, F32),
            jax.ShapeDtypeStruct(tracers.shape, F32),
            jax.ShapeDtypeStruct((SLOT_DEV, lev_dev, nlon), F32),
        ),
        in_specs=[hbm] * 13,
        out_specs=(hbm, hbm, vmem),
        scratch_shapes=[
            pltpu.VMEM((4, rows_dev, nlon), F32),
            pltpu.VMEM((fields - 1, 4, rows_dev, nlon), F32),
            pltpu.VMEM((3, rows_dev, nlon), F32),
            pltpu.VMEM((2, rows_dev, nlon), F32),
            pltpu.VMEM((2, rows_dev, nlon), F32),
            pltpu.VMEM((2, padded, padded), BF16),
            pltpu.VMEM((2, padded, padded), BF16),
            pltpu.VMEM((rows_dev, 128), F32),
            pltpu.VMEM((8, 2 * padded), F32),
            pltpu.VMEM((CHUNK, CHUNK), BF16),
            pltpu.VMEM((1, flags.shape[0]), jnp.int32),
            pltpu.SMEM(flags.shape, jnp.int32),
            pltpu.SMEM(flags.shape, jnp.int32),
            pltpu.VMEM((2, 16, nlon), F32),
            pltpu.VMEM((2, 16, nlon), F32),
            pltpu.VMEM((2, 16, nlon), F32),
            pltpu.VMEM((2, 16, nlon), F32),
            pltpu.VMEM((rows_dev, 2 * padded), F32),
            pltpu.VMEM((count, nlon), F32),
            pltpu.VMEM((2, 2 * count, padded), BF16),
            pltpu.VMEM((2, 2 * count, padded), BF16),
            pltpu.VMEM((2, count, padded), F32),
            pltpu.VMEM((rows_dev, nlon), F32),
            pltpu.VMEM((2, lat_count, cap, nlon), F32),
            pltpu.VMEM((2, lat_count, cap, nlon), F32),
            pltpu.VMEM((2, fields, rows_dev, nlon), F32),
            dma((13,)),
            dma((5,)),
            dma((5,)),
            dma((2,)),
            dma((2,)),
            dma((2, lat_count)),
            dma((2, lat_count)),
            dma((2,)),
            dma((2, 2)),
        ],
        compiler_params=pltpu.CompilerParams(
            collective_id=0, has_side_effects=True, vmem_limit_bytes=56 * 1024 * 1024
        ),
    )(thickness, tracers, east, north, vert, flags, slots, slots.reshape(1, -1), *tables)


def solution(mesh):
    def run(thickness, tracers, east, north, vert, flags, slots):
        total_rows, nlon = thickness.shape[1:]
        high, low = spectral_table(nlon)
        cells = P("lev", "lat", None)
        mapped = jax.shard_map(
            local,
            mesh=mesh,
            in_specs=(cells, P(None, "lev", "lat", None), cells, cells, cells) + (P(),) * 7,
            out_specs=(cells, P(None, "lev", "lat", None), P("lat", "lev", None)),
            check_vma=False,
        )
        tables = (high, low, row_constants(total_rows), sine_rows(nlon), interleave())
        return mapped(
            thickness, tracers, east, north, vert, flags, slots, *(jnp.asarray(t) for t in tables)
        )

    return run
```
